768 devices in a mesh: row: 12 (over z), col: 2 (over core), layer: 32 (over y, x).
Axes of the slice: x: 4, y: 8, z: 12, core: 2. Of those that a mesh axis runs over, the one named last changes fastest.
Arguments:
- a_panel: bfloat16 [12288, 131072], P('row', ('col', 'layer')), may hold values from -6 to 6
- b_panel: bfloat16 [131072, 768], P(('col', 'layer'), 'row'), may hold values from -0.046875 to 0.046875
- a_occ: int32 [96, 1024], P('row', ('col', 'layer')), may hold values 0 or 1
- b_occ: int32 [1024, 6], P(('col', 'layer')), may hold values 0 or 1
Outputs:
- product: float32 [12288, 768], P('row', ('col', 'layer'))
The draws below stay inside these ranges and needn't reach their ends.
All inputs are finite; a program needn't handle non-finite values. No bound on the sum of `a_occ` or of `b_occ` on one device may be relied on, other than what follows from the above.
Results may differ from the reference program's by a relative error of at most 0.0003.
Values may be sent and summed in bfloat16 or wider, within the bound.
A program may use at most 32 MiB of HBM per device.

```python
import jax
import jax.numpy as jnp

BS = 128
NB = 6
M = 12288
K = 131072
N = 768


def plant(array, own_key, least, high):
    longest = array.shape.index(max(array.shape))
    spots = []
    for shift in (0, 1):
        where = [jax.random.randint(jax.random.fold_in(own_key, axis), (), 0, length) for axis, length in enumerate(array.shape)]
        where[longest] = (where[longest] + shift) % array.shape[longest]
        spots.append(tuple(where))
    return array.at[spots[0]].set(least).at[spots[1]].set(high)


def level_of(stream_key, dims, cuts, least, top_value):
    def one(axis_at, parts):
        heights = jax.random.uniform(jax.random.fold_in(jax.random.fold_in(stream_key, 6), axis_at), (parts,), jnp.float32, least / len(cuts), top_value / len(cuts))
        return jnp.repeat(jnp.exp(heights), dims[axis_at] // parts).reshape((-1,) + (1,) * (len(dims) - axis_at - 1))

    factor_of = one(*cuts[0])
    for cut in cuts[1:]:
        factor_of = factor_of * one(*cut)
    return factor_of


def normal_values(own_key, dims, spread, limit, shards=(), dtype=jnp.bfloat16):
    result = jax.random.normal(own_key, dims, jnp.float32) * spread
    if len(shards) > 0:
        result = level_of(own_key, dims, shards, -0.22, 0.18) * result
    return jnp.clip(result, min=-limit, max=limit).astype(dtype)


def setup_inputs(seed: int = 0) -> dict:
    key_list = jax.random.split(jax.random.key(seed), 5)
    a_panel = normal_values(key_list[0], (M, K), 1.0, 6.0, ((0, 12), (1, 64)))
    b_panel = normal_values(key_list[1], (K, N), (K // 8) ** -0.5, 0.046875, ((0, 64), (1, 12)))
    a_occ = plant((jax.random.randint(key_list[2], (M // BS, K // BS), 0, 8) < 1).astype(jnp.int32), jax.random.fold_in(key_list[2], 1), 0, 1)
    b_occ = plant((jax.random.randint(key_list[3], (K // BS, NB), 0, 8) < 1).astype(jnp.int32), jax.random.fold_in(key_list[3], 1), 0, 1)
    return {"a_panel": a_panel, "b_panel": b_panel, "a_occ": a_occ, "b_occ": b_occ}


def expand(occupancy, block):
    return jnp.repeat(jnp.repeat(occupancy, block, 0), block, 1).astype(jnp.bfloat16)


def reference(a_panel, b_panel, a_occ, b_occ):
    masked_a = a_panel * expand(a_occ, BS)
    masked_b = b_panel * expand(b_occ, BS)
    return jnp.dot(masked_a, masked_b, preferred_element_type=jnp.float32)
```

```python
import functools

import jax
import jax.numpy as jnp
from jax import lax
from jax.experimental import pallas as pl
from jax.experimental.pallas import tpu as pltpu
from jax.sharding import PartitionSpec as P

MESH = pl.DeviceIdType.MESH
UNIT = 4


def kernel(nz, ny, nx, a_hbm, b_hbm, aocc, bocc, out, a_v, buf, part, core_in, x_in,
           y_out, y_in, fin, load_sem, ring_tx, ring_rx, first_tx, core_tx, core_rx,
           x_tx, x_rx, y_tx, y_rx):
    layers = ny * nx
    z, c, l = (lax.axis_index(name) for name in ("row", "col", "layer"))
    y, x = l // nx, lax.rem(l, nx)
    right, left = lax.rem(z + 1, nz), lax.rem(z + nz - 1, nz)
    ring = (right, left)
    rows, depth = a_v.shape
    half = buf.shape[2]
    units = half // UNIT
    upx = units // nx
    upd = out.shape[0] // UNIT
    lines = rows // 128
    per_unit = UNIT * lines
    per_x = upx * per_unit

    load_a = pltpu.make_async_copy(a_hbm, a_v, load_sem.at[0])
    load_b = [
        pltpu.make_async_copy(b_hbm.at[pl.ds((1 - d) * half, half)], buf.at[0, d], load_sem.at[1 + d])
        for d in range(2)
    ]
    for copy in load_b:
        copy.start()
    load_a.start()

    barrier = pltpu.get_barrier_semaphore()

    def greet(device):
        pl.semaphore_signal(barrier, inc=1, device_id=device, device_id_type=MESH)

    greet((right, c, l))
    greet((left, c, l))
    greet((z, 1 - c, l))

    def greet_layer(i, _):
        greet((z, c, lax.rem(l + i, layers)))
        return 0

    lax.fori_loop(1, layers, greet_layer, 0)

    def factor(value):
        return jnp.full((16, 128), value.astype(jnp.float32), jnp.float32).astype(jnp.bfloat16)

    for copy in load_b:
        copy.wait()
    for k in range(depth // 128):
        mask = factor(bocc[(z * 2 * half) // 128, k])
        for d in range(2):
            for r in range(0, half, 16):
                spot = (0, d, pl.ds(r, 16), pl.ds(k * 128, 128))
                buf[spot] = buf[spot] * mask

    pl.semaphore_wait(barrier, layers + 2)

    def ring_copy(g, d, source=None, tx=None, ahead=2):
        return pltpu.make_async_remote_copy(
            src_ref=buf.at[g, d] if source is None else source,
            dst_ref=buf.at[g + ahead, d],
            send_sem=ring_tx.at[g, d] if tx is None else tx,
            recv_sem=ring_rx.at[g + ahead, d],
            device_id=(ring[d], c, l),
            device_id_type=MESH,
        )

    def first_copy(d):
        return ring_copy(0, d, source=buf.at[0, 1 - d], tx=first_tx.at[d], ahead=1)

    for d in range(2):
        first_copy(d).start()
    for d in range(2):
        ring_copy(0, d).start()

    load_a.wait()

    def mask_a(k, _):
        cols = pl.ds(pl.multiple_of(k * 128, 128), 128)
        for i in range(rows // 128):
            mask = factor(aocc[i, k])
            tile = a_v[pl.ds(i * 128, 128), cols].reshape(8, 16, 128)
            a_v[pl.ds(i * 128, 128), cols] = (tile * mask[None]).reshape(128, 128)
        return 0

    lax.fori_loop(0, depth // 128, mask_a, 0)

    def meta(g, d):
        s = (g + 1) // 2
        if d == 0:
            j, h = lax.rem(z - s + nz, nz), lax.rem(g + 1, 2)
        else:
            j, h = lax.rem(z + s, nz), lax.rem(g, 2)
        return 2 * j + h

    def is_mine(g, d):
        return meta(g, d) // nz == c

    def core_copy(g, d):
        return pltpu.make_async_remote_copy(
            src_ref=part.at[g, d], dst_ref=core_in.at[g, d],
            send_sem=core_tx.at[g, d], recv_sem=core_rx.at[g, d],
            device_id=(z, 1 - c, l), device_id_type=MESH,
        )

    def x_copy(g, d, i):
        to = lax.rem(x + i, nx)
        return pltpu.make_async_remote_copy(
            src_ref=part.at[g, d, pl.ds(pl.multiple_of(to * per_x, 8), per_x)],
            dst_ref=x_in.at[g, d, i - 1],
            send_sem=x_tx.at[g, d, i - 1], recv_sem=x_rx.at[g, d, i - 1],
            device_id=(z, c, y * nx + to), device_id_type=MESH,
        )

    def y_copy(g, d, i):
        unit = units * lax.rem(meta(g, d), nz) + x * upx + i
        owner, u = unit // upd, lax.rem(unit, upd)
        copy = pltpu.make_async_remote_copy(
            src_ref=y_out.at[g, d, pl.ds(i * per_unit, per_unit)],
            dst_ref=y_in.at[u, y],
            send_sem=y_tx.at[g, d, i], recv_sem=y_rx.at[u, y],
            device_id=(z, c, owner), device_id_type=MESH,
        )
        return copy, owner, u

    def compute(g):
        lhs = buf[g].reshape(2 * half, depth)
        for m in range(0, rows, 256):
            sums = lax.dot_general(
                lhs, a_v[pl.ds(m, 256), :], (((1,), (1,)), ((), ())),
                preferred_element_type=jnp.float32,
            )
            for d in range(2):
                for n in range(2):
                    part[g, d, pl.ds(m // 128 + n, half, stride=lines), :] = (
                        sums[d * half:(d + 1) * half, n * 128:(n + 1) * 128]
                    )
        for d in range(2):
            @pl.when(jnp.logical_not(is_mine(g, d)))
            def _():
                core_copy(g, d).start()

    def add_core(g):
        for d in range(2):
            @pl.when(is_mine(g, d))
            def _():
                core_copy(g, d).wait_recv()
                part[g, d] = part[g, d] + core_in[g, d]
                for i in range(1, nx):
                    x_copy(g, d, i).start()

    def add_x(g):
        for d in range(2):
            @pl.when(is_mine(g, d))
            def _():
                total = part[g, d, pl.ds(pl.multiple_of(x * per_x, 8), per_x), :]
                for i in range(1, nx):
                    x_copy(g, d, i).wait_recv()
                    total = total + x_in[g, d, i - 1]
                y_out[g, d] = total
                for i in range(upx):
                    copy, owner, u = y_copy(g, d, i)

                    @pl.when(owner == l)
                    def _():
                        y_in[u, y] = y_out[g, d, pl.ds(i * per_unit, per_unit), :]

                    @pl.when(owner != l)
                    def _():
                        copy.start()

    def drain(g):
        for d in range(2):
            @pl.when(g < nz - 2)
            def _():
                ring_copy(g, d).wait_send()

            mine = is_mine(g, d)

            @pl.when(jnp.logical_not(mine))
            def _():
                core_copy(g, d).wait_send()

            @pl.when(mine)
            def _():
                for i in range(1, nx):
                    x_copy(g, d, i).wait_send()
                for i in range(upx):
                    copy, owner, _u = y_copy(g, d, i)

                    @pl.when(owner != l)
                    def _():
                        copy.wait_send()

    def step(g, _):
        for d in range(2):
            @pl.when(g > 0)
            def _():
                pltpu.make_async_copy(buf.at[g, d], buf.at[g, d], ring_rx.at[g, d]).wait()

            @pl.when(jnp.logical_and(g > 0, g < nz - 2))
            def _():
                ring_copy(g, d).start()

        compute(g)

        @pl.when(g >= 1)
        def _():
            add_core(g - 1)

        @pl.when(g >= 2)
        def _():
            add_x(g - 2)

        @pl.when(g >= 3)
        def _():
            drain(g - 3)

        return 0

    lax.fori_loop(0, nz, step, 0)
    add_core(nz - 1)
    add_x(nz - 2)
    add_x(nz - 1)
    for g in range(nz - 3, nz):
        drain(g)
    for d in range(2):
        first_copy(d).wait_send()

    for u in range(upd):
        unit = l * upd + u
        via = lax.rem(unit, units) // upx
        for i in range(ny):
            @pl.when(jnp.logical_not(jnp.logical_and(via == x, i == y)))
            def _():
                pltpu.make_async_copy(y_in.at[u, i], y_in.at[u, i], y_rx.at[u, i]).wait()
        total = y_in[u, 0]
        for i in range(1, ny):
            total = total + y_in[u, i]
        fin[pl.ds(u * per_unit, per_unit), :] = total
    for n in range(lines):
        out[:, pl.ds(n * 128, 128)] = fin[pl.ds(n, out.shape[0], stride=lines), :]


def body(nz, ny, nx, a_panel, b_panel, a_occ, b_occ):
    rows, depth = a_panel.shape
    half = b_panel.shape[1] // 2
    owned = nz * half // (ny * nx)
    lines = rows // 128
    units = half // UNIT
    upx = units // nx
    upd = owned // UNIT
    dma = pltpu.SemaphoreType.DMA
    result = pl.pallas_call(
        functools.partial(kernel, nz, ny, nx),
        out_shape=jax.ShapeDtypeStruct((owned, rows), jnp.float32),
        in_specs=[
            pl.BlockSpec(memory_space=pl.ANY),
            pl.BlockSpec(memory_space=pl.ANY),
            pl.BlockSpec(memory_space=pltpu.SMEM),
            pl.BlockSpec(memory_space=pltpu.SMEM),
        ],
        out_specs=pl.BlockSpec(memory_space=pltpu.VMEM),
        scratch_shapes=[
            pltpu.VMEM((rows, depth), jnp.bfloat16),
            pltpu.VMEM((nz, 2, half, depth), jnp.bfloat16),
            pltpu.VMEM((nz, 2, half * lines, 128), jnp.float32),
            pltpu.VMEM((nz, 2, half * lines, 128), jnp.float32),
            pltpu.VMEM((nz, 2, nx - 1, upx * UNIT * lines, 128), jnp.float32),
            pltpu.VMEM((nz, 2, upx * UNIT * lines, 128), jnp.float32),
            pltpu.VMEM((upd, ny, UNIT * lines, 128), jnp.float32),
            pltpu.VMEM((owned * lines, 128), jnp.float32),
            dma((3,)),
            dma((nz, 2)),
            dma((nz, 2)),
            dma((2,)),
            dma((nz, 2)),
            dma((nz, 2)),
            dma((nz, 2, nx - 1)),
            dma((nz, 2, nx - 1)),
            dma((nz, 2, upx)),
            dma((upd, ny)),
        ],
        compiler_params=pltpu.CompilerParams(
            collective_id=0, has_side_effects=True, vmem_limit_bytes=48 * 1024 * 1024
        ),
        cost_estimate=pl.CostEstimate(
            flops=2 * rows * depth * nz * 2 * half, bytes_accessed=rows * depth * 2, transcendentals=0
        ),
    )(a_panel, b_panel.T, a_occ, b_occ.T)
    return result.T


def solution(mesh):
    nz, layers = mesh.shape["row"], mesh.shape["layer"]
    nx = 4 if layers % 4 == 0 and layers > 4 else 2
    in_specs = (
        P("row", ("col", "layer")),
        P(("col", "layer"), "row"),
        P("row", ("col", "layer")),
        P(("col", "layer"), None),
    )
    out_specs = P("row", ("col", "layer"))
    return jax.shard_map(
        functools.partial(body, nz, layers // nx, nx),
        mesh=mesh, in_specs=in_specs, out_specs=out_specs, check_vma=False,
    )
```

```python
import functools

import jax
import jax.numpy as jnp
from jax import lax
from jax.experimental import pallas as pl
from jax.experimental.pallas import tpu as pltpu
from jax.sharding import PartitionSpec as P

MESH = pl.DeviceIdType.MESH
BLOCK = 128
NX, NY = 4, 8


def ring_order(nz):
    if nz == 12:
        names = ["o0", "b1", "b2", "f1", "b3", "b4", "f2", "b5", "f3", "b6", "f4", "b7"]
    else:
        back = nz // 2
        names = ["o0"] + [n + str(s) for s in range(1, back + 1) for n in "bf" if s <= (nz - 1 - back if n == "f" else back)]
    items = [(n[0], int(n[1:])) for n in names]
    place = {item: i for i, item in enumerate(items)}
    offsets = [s if n != "f" else nz - s for n, s in items]
    onward = [place.get((n, s + 1), 0) for n, s in items]
    forward = [int(n == "f") for n, s in items]
    return offsets, onward, forward, place[("f", 1)], place[("b", 1)]


def pick(i, values):
    result = jnp.int32(values[0])
    for k, value in enumerate(values):
        if k > 0:
            result = jnp.where(i == k, jnp.int32(value), result)
    return result


def kernel(nz, slots, a_hbm, b_hbm, aocc_hbm, bocc_hbm, out, flag_out, a_v, b_v, aocc, bocc, stored, absent, wide, buf,
           part, core_in, x1_in, x2_in, y_out, y_in, f_out, fin, flag, flag_c, flag_x, flag_y,
           load_sem, own_tx, ring_tx, ring_rx, core_tx, core_rx, x1_tx, x1_rx, x2_tx, x2_rx,
           y_tx, y_rx, f_tx, f_rx, fc_tx, fc_rx, fx_tx, fx_rx, fy_tx, fy_rx):
    offsets, onward, forward, first_f, first_b = ring_order(nz)
    layers = NX * NY
    z, c, l = (lax.axis_index(name) for name in ("row", "col", "layer"))
    y, x = l // NX, lax.rem(l, NX)
    right, left = lax.rem(z + 1, nz), lax.rem(z + nz - 1, nz)
    rows, depth = a_v.shape
    width = b_v.shape[0]
    half = width // 2
    blocks = depth // BLOCK
    lines = rows // 128
    piece = width // NX * lines
    pair = piece // NY
    owned = out.shape[0]

    loads = [
        pltpu.make_async_copy(bocc_hbm, bocc, load_sem.at[0]),
        pltpu.make_async_copy(b_hbm, b_v, load_sem.at[1]),
        pltpu.make_async_copy(aocc_hbm, aocc, load_sem.at[2]),
        pltpu.make_async_copy(a_hbm, a_v, load_sem.at[3]),
    ]
    for copy in loads:
        copy.start()

    barrier = pltpu.get_barrier_semaphore()

    def greet(device):
        pl.semaphore_signal(barrier, inc=1, device_id=device, device_id_type=MESH)

    greet((right, c, l))
    greet((left, c, l))
    greet((z, 1 - c, l))

    def greet_layer(i, _):
        greet((z, c, lax.rem(l + i, layers)))
        return 0

    lax.fori_loop(1, layers, greet_layer, 0)

    def factor(value):
        return jnp.full((16, 128), value.astype(jnp.float32), jnp.float32).astype(jnp.bfloat16)

    own_column = (z * width) // BLOCK

    def note_blocks(n, over):
        count = jnp.int32(0)
        for k in range(blocks):
            stored[n, k] = factor(bocc[n, k])
            absent[n, k] = factor(1 - bocc[n, k])
            count = count + bocc[n, k]
        return over + jnp.maximum(count - slots, 0)

    loads[0].wait()
    note_blocks(own_column, jnp.int32(0))

    loads[1].wait()
    tiles = (width // 16, 16, BLOCK)
    held = [jnp.zeros(tiles, jnp.bfloat16)] * slots
    for k in reversed(range(blocks)):
        on, off = stored[own_column, k][None], absent[own_column, k][None]
        tile = b_v[:, k * BLOCK:(k + 1) * BLOCK].reshape(tiles)
        held = [(tile if s == 0 else held[s - 1]) * on + held[s] * off for s in range(slots)]
    for s in range(slots):
        buf[0, :, s * BLOCK:(s + 1) * BLOCK] = held[s].reshape(width, BLOCK)

    def mask_a(k, _):
        cols = pl.ds(pl.multiple_of(k * BLOCK, BLOCK), BLOCK)
        for i in range(rows // BLOCK):
            mask = factor(aocc[i, k])
            tile = a_v[pl.ds(i * BLOCK, BLOCK), cols].reshape(BLOCK // 16, 16, BLOCK)
            a_v[pl.ds(i * BLOCK, BLOCK), cols] = (tile * mask[None]).reshape(BLOCK, BLOCK)
        return 0

    def prepare():
        loads[2].wait()
        loads[3].wait()
        lax.fori_loop(0, blocks, mask_a, 0)
        over = lax.fori_loop(0, bocc.shape[0], note_blocks, jnp.int32(0))
        flag[0] = jnp.full(flag.shape[1:], over.astype(jnp.float32), jnp.float32)

    early = z < nz // 2
    pl.when(early)(prepare)
    pl.semaphore_wait(barrier, layers + 2)

    def ring_copy(i, h, to, device, tx):
        return pltpu.make_async_remote_copy(
            src_ref=buf.at[i, pl.ds(h * half, half)], dst_ref=buf.at[to, pl.ds(h * half, half)],
            send_sem=tx, recv_sem=ring_rx.at[to, h],
            device_id=(device, c, l), device_id_type=MESH,
        )

    def onward_copy(i, h):
        device = jnp.where(pick(i, forward) > 0, right, left)
        return ring_copy(i, h, pick(i, onward), device, ring_tx.at[i, h])

    own_copies = [ring_copy(0, h, first_b, left, own_tx.at[0, h]) for h in range(2)]
    own_copies += [ring_copy(0, h, first_f, right, own_tx.at[1, h]) for h in range(2)]
    for copy in own_copies:
        copy.start()

    flag_core = pltpu.make_async_remote_copy(
        src_ref=flag.at[0], dst_ref=flag_c, send_sem=fc_tx, recv_sem=fc_rx,
        device_id=(z, 1 - c, l), device_id_type=MESH,
    )

    def flag_copies(i, inbox, count, tx, rx, device):
        return [
            pltpu.make_async_remote_copy(
                src_ref=flag.at[i], dst_ref=inbox.at[n - 1], send_sem=tx.at[n - 1], recv_sem=rx.at[n - 1],
                device_id=(z, c, device(n)), device_id_type=MESH,
            )
            for n in range(1, count)
        ]

    flag_xs = flag_copies(1, flag_x, NX, fx_tx, fx_rx, lambda n: y * NX + lax.rem(x + n, NX))
    flag_ys = flag_copies(2, flag_y, NY, fy_tx, fy_rx, lambda n: lax.rem(y + n, NY) * NX + x)

    pl.when(jnp.logical_not(early))(prepare)
    flag_core.start()

    def shard(i):
        return lax.rem(z + pick(i, offsets), nz)

    def is_mine(i):
        return shard(i) // (nz // 2) == c

    def lines_of(p, start, size):
        return pl.ds(pl.multiple_of(p * piece + start, 8), size)

    x_right, x_left, x_far = (lax.rem(x + n, NX) for n in (1, NX - 1, 2))

    def core_copy(i):
        return pltpu.make_async_remote_copy(
            src_ref=part.at[i], dst_ref=core_in.at[i], send_sem=core_tx.at[i], recv_sem=core_rx.at[i],
            device_id=(z, 1 - c, l), device_id_type=MESH,
        )

    def x1_copies(i):
        return [
            pltpu.make_async_remote_copy(
                src_ref=part.at[i, lines_of(x_far, n * piece // 2, piece // 2)], dst_ref=x1_in.at[i, n],
                send_sem=x1_tx.at[i, n], recv_sem=x1_rx.at[i, n],
                device_id=(z, c, y * NX + to), device_id_type=MESH,
            )
            for n, to in enumerate((x_right, x_left))
        ]

    def x2_copies(i):
        return [
            pltpu.make_async_remote_copy(
                src_ref=part.at[i, lines_of(to, 0, piece)], dst_ref=x2_in.at[i, n],
                send_sem=x2_tx.at[i, n], recv_sem=x2_rx.at[i, n],
                device_id=(z, c, y * NX + to), device_id_type=MESH,
            )
            for n, to in enumerate((x_right, x_left))
        ]

    def y_copies(i):
        copies = []
        for n in range(1, NY):
            to = lax.rem(y + n, NY)
            copies.append(pltpu.make_async_remote_copy(
                src_ref=y_out.at[i, pl.ds(pl.multiple_of(to * pair, 8), pair)], dst_ref=y_in.at[i, n - 1],
                send_sem=y_tx.at[i, n - 1], recv_sem=y_rx.at[i, n - 1],
                device_id=(z, c, to * NX + x), device_id_type=MESH,
            ))
        return copies

    def f_copy(i):
        column = width * lax.rem(shard(i), nz // 2) + (width // NX) * x + (pair // lines) * y
        owner, spot = column // owned, lax.rem(column, owned) // (pair // lines)
        copy = pltpu.make_async_remote_copy(
            src_ref=f_out.at[i], dst_ref=fin.at[pl.ds(pl.multiple_of(spot * pair, 8), pair)],
            send_sem=f_tx.at[i], recv_sem=f_rx.at[spot],
            device_id=(z, c, owner), device_id_type=MESH,
        )
        return copy, owner, spot

    def compute(i):
        column = (shard(i) * width) // BLOCK
        held = [buf[i, :, s * BLOCK:(s + 1) * BLOCK].reshape(tiles) for s in range(slots)]
        for k in range(blocks):
            on, off = stored[column, k][None], absent[column, k][None]
            wide[:, k * BLOCK:(k + 1) * BLOCK] = (held[0] * on).reshape(width, BLOCK)
            held = [
                held[s] * off + held[s + 1] * on if s < slots - 1 else held[s] * off
                for s in range(min(slots, blocks - 1 - k))
            ]
        lhs = wide[...]
        for m in range(0, rows, 256):
            sums = lax.dot_general(
                lhs, a_v[pl.ds(m, 256), :], (((1,), (1,)), ((), ())), preferred_element_type=jnp.float32,
            )
            for n in range(2):
                part[i, pl.ds(m // 128 + n, width, stride=lines), :] = sums[:, n * 128:(n + 1) * 128]

        @pl.when(jnp.logical_not(is_mine(i)))
        def _():
            core_copy(i).start()

    def add_core(i):
        @pl.when(is_mine(i))
        def _():
            core_copy(i).wait_recv()
            part[i] = part[i] + core_in[i]
            for copy in x1_copies(i):
                copy.start()

    def add_x1(i):
        @pl.when(is_mine(i))
        def _():
            copies, later = x1_copies(i), x2_copies(i)
            for n, to in enumerate((x_right, x_left)):
                copies[n].wait_recv()
                spot = lines_of(to, n * piece // 2, piece // 2)
                part[i, spot, :] = part[i, spot, :] + x1_in[i, n]
                later[n].start()

    def add_x2(i):
        @pl.when(is_mine(i))
        def _():
            for copy in x2_copies(i):
                copy.wait_recv()
            y_out[i] = part[i, lines_of(x, 0, piece), :] + (x2_in[i, 0] + x2_in[i, 1])
            for copy in y_copies(i):
                copy.start()

    def add_y(i):
        @pl.when(is_mine(i))
        def _():
            total = y_out[i, pl.ds(pl.multiple_of(y * pair, 8), pair), :]
            for n, copy in enumerate(y_copies(i)):
                copy.wait_recv()
                total = total + y_in[i, n]
            copy, owner, spot = f_copy(i)
            f_out[i] = total

            @pl.when(owner == l)
            def _():
                fin[pl.ds(pl.multiple_of(spot * pair, 8), pair), :] = total

            @pl.when(owner != l)
            def _():
                copy.start()

    def drain(i):
        @pl.when(pick(i, onward) > 0)
        def _():
            for h in range(2):
                onward_copy(i, h).wait_send()

        mine = is_mine(i)

        @pl.when(jnp.logical_not(mine))
        def _():
            core_copy(i).wait_send()

        @pl.when(mine)
        def _():
            for copy in x1_copies(i) + x2_copies(i) + y_copies(i):
                copy.wait_send()
            copy, owner, _spot = f_copy(i)

            @pl.when(owner != l)
            def _():
                copy.wait_send()

    stages = ((1, add_core), (3, add_x1), (5, add_x2), (8, add_y))

    def step(i, _):
        @pl.when(i > 0)
        def _():
            for h in range(2):
                spot = buf.at[i, pl.ds(h * half, half)]
                pltpu.make_async_copy(spot, spot, ring_rx.at[i, h]).wait()

                @pl.when(pick(i, onward) > 0)
                def _():
                    onward_copy(i, h).start()

        compute(i)
        for lag, stage in stages:
            @pl.when(i >= lag)
            def _():
                stage(i - lag)

        return 0

    lax.fori_loop(0, nz - 2, step, 0)

    flag_core.wait()
    flag[1] = flag[0] + flag_c[...]
    for copy in flag_xs:
        copy.start()
    lax.fori_loop(nz - 2, nz - 1, step, 0)
    total_x = flag[1]
    for n, copy in enumerate(flag_xs):
        copy.wait()
        total_x = total_x + flag_x[n]
    flag[2] = total_x
    for copy in flag_ys:
        copy.start()
    lax.fori_loop(nz - 1, nz, step, 0)

    def catch_up(k, low, high):
        for i in range(max(low, 0), high):
            stages[k][1](i)

    left_over = [nz - lag for lag, _stage in stages]
    add_core(nz - 1)
    catch_up(1, left_over[1], nz - 1)
    catch_up(2, left_over[2], nz - 3)
    catch_up(3, left_over[3], nz - 6)
    add_x1(nz - 1)
    catch_up(2, max(left_over[2], nz - 3), nz - 1)
    catch_up(3, max(left_over[3], nz - 6), nz - 4)
    add_x2(nz - 1)
    catch_up(3, max(left_over[3], nz - 4), nz - 1)
    for i in range(nz - 1):
        drain(i)
    add_y(nz - 1)
    drain(nz - 1)
    total_y = flag[2]
    for n, copy in enumerate(flag_ys):
        copy.wait()
        total_y = total_y + flag_y[n]
    flag_out[...] = total_y
    for copy in own_copies:
        copy.wait_send()

    for spot in range(owned * lines // pair):
        column = lax.rem(l * owned + spot * (pair // lines), width)
        from_x, from_y = column // (width // NX), lax.rem(column, width // NX) // (pair // lines)

        @pl.when(jnp.logical_not(jnp.logical_and(from_x == x, from_y == y)))
        def _():
            here = fin.at[pl.ds(spot * pair, pair)]
            pltpu.make_async_copy(here, here, f_rx.at[spot]).wait()
    for n in range(lines):
        out[:, pl.ds(n * 128, 128)] = fin[pl.ds(n, owned, stride=lines), :]


def sparse_product(nz, a_panel, b_panel, a_occ, b_occ):
    rows, depth = a_panel.shape
    width = b_panel.shape[1]
    blocks = depth // BLOCK
    slots = blocks // 2
    lines = rows // 128
    owned = nz * width // (2 * NX * NY)
    piece = width // NX * lines
    pair = piece // NY
    columns = b_occ.shape[1]
    dma = pltpu.SemaphoreType.DMA
    f32, bf16 = jnp.float32, jnp.bfloat16
    scratch = [
        pltpu.VMEM((rows, depth), bf16),
        pltpu.VMEM((width, depth), bf16),
        pltpu.SMEM(a_occ.shape, jnp.int32),
        pltpu.SMEM((columns, blocks), jnp.int32),
        pltpu.VMEM((columns, blocks, 16, BLOCK), bf16),
        pltpu.VMEM((columns, blocks, 16, BLOCK), bf16),
        pltpu.VMEM((width, depth), bf16),
        pltpu.VMEM((nz, width, slots * BLOCK), bf16),
        pltpu.VMEM((nz, width * lines, 128), f32),
        pltpu.VMEM((nz, width * lines, 128), f32),
        pltpu.VMEM((nz, 2, piece // 2, 128), f32),
        pltpu.VMEM((nz, 2, piece, 128), f32),
        pltpu.VMEM((nz, piece, 128), f32),
        pltpu.VMEM((nz, NY - 1, pair, 128), f32),
        pltpu.VMEM((nz, pair, 128), f32),
        pltpu.VMEM((owned * lines, 128), f32),
        pltpu.VMEM((3, 8, 128), f32),
        pltpu.VMEM((8, 128), f32),
        pltpu.VMEM((NX - 1, 8, 128), f32),
        pltpu.VMEM((NY - 1, 8, 128), f32),
        dma((4,)), dma((2, 2)), dma((nz, 2)), dma((nz, 2)),
        dma((nz,)), dma((nz,)), dma((nz, 2)), dma((nz, 2)), dma((nz, 2)), dma((nz, 2)),
        dma((nz, NY - 1)), dma((nz, NY - 1)), dma((nz,)), dma((owned * lines // pair,)),
        dma(()), dma(()), dma((NX - 1,)), dma((NX - 1,)), dma((NY - 1,)), dma((NY - 1,)),
    ]
    anywhere = pl.BlockSpec(memory_space=pl.ANY)
    inside = pl.BlockSpec(memory_space=pltpu.VMEM)
    return pl.pallas_call(
        functools.partial(kernel, nz, slots),
        out_shape=(jax.ShapeDtypeStruct((owned, rows), f32), jax.ShapeDtypeStruct((8, 128), f32)),
        in_specs=[anywhere] * 4,
        out_specs=(inside, inside),
        scratch_shapes=scratch,
        compiler_params=pltpu.CompilerParams(
            collective_id=0, has_side_effects=True, vmem_limit_bytes=60 * 1024 * 1024
        ),
        cost_estimate=pl.CostEstimate(
            flops=2 * rows * slots * BLOCK * nz * width, bytes_accessed=rows * depth * 2, transcendentals=0
        ),
    )(a_panel, b_panel.T, a_occ, b_occ.T)


def expand(occupancy, block):
    return jnp.repeat(jnp.repeat(occupancy, block, 0), block, 1).astype(jnp.bfloat16)


def dense_product(nz, a_panel, b_panel, a_occ, b_occ):
    z = lax.axis_index("row")
    width, depth = b_panel.shape[1], b_panel.shape[0]

    def step(s, carry):
        held, gathered = carry
        gathered = lax.dynamic_update_slice(gathered, held[None], (lax.rem(z - s + nz, nz), 0, 0))
        return lax.ppermute(held, "row", [(i, (i + 1) % nz) for i in range(nz)]), gathered

    occupied = lax.dynamic_slice_in_dim(b_occ.T, (z * width) // BLOCK, 1).astype(b_panel.dtype)
    start = (b_panel.T * jnp.repeat(occupied, BLOCK, 1), jnp.zeros((nz, width, depth), b_panel.dtype))
    _, gathered = lax.fori_loop(0, nz, step, start)
    terms = lax.dot_general(
        gathered.reshape(nz * width, depth),
        a_panel * expand(a_occ, BLOCK),
        (((1,), (1,)), ((), ())), preferred_element_type=jnp.float32,
    )
    shares = 2 * NX * NY
    terms = terms.reshape(shares, nz * width // shares, a_panel.shape[0])
    return lax.all_to_all(terms, ("col", "layer"), 0, 0).sum(0).T


def body(nz, a_panel, b_panel, a_occ, b_occ):
    result, over = sparse_product(nz, a_panel, b_panel, a_occ, b_occ)
    return lax.cond(
        over[0, 0] > 0,
        lambda: dense_product(nz, a_panel, b_panel, a_occ, b_occ),
        lambda: result.T,
    )


def solution(mesh):
    in_specs = (
        P("row", ("col", "layer")),
        P(("col", "layer"), "row"),
        P("row", ("col", "layer")),
        P(("col", "layer"), None),
    )
    out_specs = P("row", ("col", "layer"))
    return jax.shard_map(
        functools.partial(body, mesh.shape["row"]),
        mesh=mesh, in_specs=in_specs, out_specs=out_specs, check_vma=False,
    )
```

```python
import functools

import jax
import jax.numpy as jnp
from jax import lax
from jax.experimental import pallas as pl
from jax.experimental.pallas import tpu as pltpu
from jax.sharding import PartitionSpec as P

MESH = pl.DeviceIdType.MESH
BLOCK = 128
UNIT = 4
NX, NY = 4, 8


def ring_order(nz):
    names = ["o0"]
    for s in range(1, nz // 2 + 1):
        names += ["b" + str(s)] + ["f" + str(s)] * (2 * s < nz)
    items = [(n[0], int(n[1:])) for n in names]
    place = {item: i for i, item in enumerate(items)}
    offsets = [s if n != "f" else nz - s for n, s in items]
    onward = [place.get((n, s + 1), 0) for n, s in items]
    forward = [int(n == "f") for n, s in items]
    return offsets, onward, forward, place[("f", 1)], place[("b", 1)]


def pick(i, values):
    result = jnp.int32(values[0])
    for k, value in enumerate(values):
        if k > 0:
            result = jnp.where(i == k, jnp.int32(value), result)
    return result


def kernel(nz, slots, a_hbm, b_hbm, aocc_hbm, bocc_hbm, out, flag_out, a_v, b_v, aocc, bocc, stored, absent, wide, buf,
           part, core_in, x1_in, x2_in, y_out, y_in, fin, flag, flag_c, flag_x, flag_y,
           load_sem, own_tx, ring_tx, ring_rx, core_tx, core_rx, x1_tx, x1_rx, x2_tx, x2_rx,
           y_tx, y_rx, fc_tx, fc_rx, fx_tx, fx_rx, fy_tx, fy_rx):
    offsets, onward, forward, first_f, first_b = ring_order(nz)
    layers = NX * NY
    z, c, l = (lax.axis_index(name) for name in ("row", "col", "layer"))
    y, x = l // NX, lax.rem(l, NX)
    right, left = lax.rem(z + 1, nz), lax.rem(z + nz - 1, nz)
    rows, depth = a_v.shape
    width = b_v.shape[0]
    half = width // 2
    blocks = depth // BLOCK
    lines = rows // 128
    piece = width // NX * lines
    unit = UNIT * lines
    units = piece // unit
    per_owner = out.shape[0] // UNIT
    pairs = nz // 2
    owned = out.shape[0]

    loads = [
        pltpu.make_async_copy(bocc_hbm, bocc, load_sem.at[0]),
        pltpu.make_async_copy(b_hbm, b_v, load_sem.at[1]),
        pltpu.make_async_copy(aocc_hbm, aocc, load_sem.at[2]),
        pltpu.make_async_copy(a_hbm, a_v, load_sem.at[3]),
    ]
    for copy in loads:
        copy.start()

    barrier = pltpu.get_barrier_semaphore()

    def greet(device):
        pl.semaphore_signal(barrier, inc=1, device_id=device, device_id_type=MESH)

    greet((right, c, l))
    greet((left, c, l))
    greet((z, 1 - c, l))

    def greet_layer(i, _):
        greet((z, c, lax.rem(l + i, layers)))
        return 0

    lax.fori_loop(1, layers, greet_layer, 0)

    def factor(value):
        return jnp.full((16, 128), value.astype(jnp.float32), jnp.float32).astype(jnp.bfloat16)

    own_column = (z * width) // BLOCK

    def note_blocks(n, over):
        count = jnp.int32(0)
        for k in range(blocks):
            stored[n, k] = factor(bocc[n, k])
            absent[n, k] = factor(1 - bocc[n, k])
            count = count + bocc[n, k]
        return over + jnp.maximum(count - slots, 0)

    loads[0].wait()
    note_blocks(own_column, jnp.int32(0))

    loads[1].wait()
    tiles = (width // 16, 16, BLOCK)
    held = [jnp.zeros(tiles, jnp.bfloat16)] * slots
    for k in reversed(range(blocks)):
        on, off = stored[own_column, k][None], absent[own_column, k][None]
        tile = b_v[:, k * BLOCK:(k + 1) * BLOCK].reshape(tiles)
        held = [(tile if s == 0 else held[s - 1]) * on + held[s] * off for s in range(slots)]
    for s in range(slots):
        buf[0, :, s * BLOCK:(s + 1) * BLOCK] = held[s].reshape(width, BLOCK)

    def mask_a(k, _):
        cols = pl.ds(pl.multiple_of(k * BLOCK, BLOCK), BLOCK)
        for i in range(rows // BLOCK):
            mask = factor(aocc[i, k])
            tile = a_v[pl.ds(i * BLOCK, BLOCK), cols].reshape(BLOCK // 16, 16, BLOCK)
            a_v[pl.ds(i * BLOCK, BLOCK), cols] = (tile * mask[None]).reshape(BLOCK, BLOCK)
        return 0

    def prepare():
        loads[2].wait()
        loads[3].wait()
        lax.fori_loop(0, blocks, mask_a, 0)
        over = lax.fori_loop(0, bocc.shape[0], note_blocks, jnp.int32(0))
        flag[0] = jnp.full(flag.shape[1:], over.astype(jnp.float32), jnp.float32)

    early = z < nz // 2
    pl.when(early)(prepare)
    pl.semaphore_wait(barrier, layers + 2)

    def ring_copy(i, h, to, device, tx):
        return pltpu.make_async_remote_copy(
            src_ref=buf.at[i, pl.ds(h * half, half)], dst_ref=buf.at[to, pl.ds(h * half, half)],
            send_sem=tx, recv_sem=ring_rx.at[to, h],
            device_id=(device, c, l), device_id_type=MESH,
        )

    def onward_copy(i, h):
        device = jnp.where(pick(i, forward) > 0, right, left)
        return ring_copy(i, h, pick(i, onward), device, ring_tx.at[i, h])

    own_copies = [ring_copy(0, h, first_b, left, own_tx.at[0, h]) for h in range(2)]
    own_copies += [ring_copy(0, h, first_f, right, own_tx.at[1, h]) for h in range(2)]
    for copy in own_copies:
        copy.start()

    flag_core = pltpu.make_async_remote_copy(
        src_ref=flag.at[0], dst_ref=flag_c, send_sem=fc_tx, recv_sem=fc_rx,
        device_id=(z, 1 - c, l), device_id_type=MESH,
    )

    def flag_copies(i, inbox, count, tx, rx, device):
        return [
            pltpu.make_async_remote_copy(
                src_ref=flag.at[i], dst_ref=inbox.at[n - 1], send_sem=tx.at[n - 1], recv_sem=rx.at[n - 1],
                device_id=(z, c, device(n)), device_id_type=MESH,
            )
            for n in range(1, count)
        ]

    flag_xs = flag_copies(1, flag_x, NX, fx_tx, fx_rx, lambda n: y * NX + lax.rem(x + n, NX))
    flag_ys = flag_copies(2, flag_y, NY, fy_tx, fy_rx, lambda n: lax.rem(y + n, NY) * NX + x)

    pl.when(jnp.logical_not(early))(prepare)
    flag_core.start()

    def shard(i):
        return lax.rem(z + pick(i, offsets), nz)

    def is_mine(i):
        return shard(i) // (nz // 2) == c

    def lines_of(p, start, size):
        return pl.ds(pl.multiple_of(p * piece + start, 8), size)

    x_right, x_left, x_far = (lax.rem(x + n, NX) for n in (1, NX - 1, 2))

    def core_copy(i):
        return pltpu.make_async_remote_copy(
            src_ref=part.at[i], dst_ref=core_in.at[i], send_sem=core_tx.at[i], recv_sem=core_rx.at[i],
            device_id=(z, 1 - c, l), device_id_type=MESH,
        )

    def x1_copies(i):
        return [
            pltpu.make_async_remote_copy(
                src_ref=part.at[i, lines_of(x_far, n * piece // 2, piece // 2)], dst_ref=x1_in.at[i, n],
                send_sem=x1_tx.at[i, n], recv_sem=x1_rx.at[i, n],
                device_id=(z, c, y * NX + to), device_id_type=MESH,
            )
            for n, to in enumerate((x_right, x_left))
        ]

    def x2_copies(i):
        return [
            pltpu.make_async_remote_copy(
                src_ref=part.at[i, lines_of(to, 0, piece)], dst_ref=x2_in.at[i, n],
                send_sem=x2_tx.at[i, n], recv_sem=x2_rx.at[i, n],
                device_id=(z, c, y * NX + to), device_id_type=MESH,
            )
            for n, to in enumerate((x_right, x_left))
        ]

    def y_copy(i, n):
        column = width * lax.rem(shard(i), nz // 2) + (width // NX) * x + UNIT * n
        owner, spot = column // owned, lax.rem(column, owned) // UNIT
        copy = pltpu.make_async_remote_copy(
            src_ref=y_out.at[i, pl.ds(n * unit, unit)], dst_ref=y_in.at[spot, y],
            send_sem=y_tx.at[i, n], recv_sem=y_rx.at[spot, y],
            device_id=(z, c, owner), device_id_type=MESH,
        )
        return copy, owner, spot

    def compute(p):
        for t in range(2):
            i = 2 * p + t
            column = (shard(i) * width) // BLOCK
            place = pl.ds(t * width, width)
            held = [buf[i, :, s * BLOCK:(s + 1) * BLOCK].reshape(tiles) for s in range(slots)]
            for k in range(blocks):
                on, off = stored[column, k][None], absent[column, k][None]
                wide[place, k * BLOCK:(k + 1) * BLOCK] = (held[0] * on).reshape(width, BLOCK)
                held = [
                    held[s] * off + held[s + 1] * on if s < slots - 1 else held[s] * off
                    for s in range(min(slots, blocks - 1 - k))
                ]
        lhs = wide[...]
        for m in range(0, rows, 256):
            sums = lax.dot_general(
                lhs, a_v[pl.ds(m, 256), :], (((1,), (1,)), ((), ())), preferred_element_type=jnp.float32,
            )
            for t in range(2):
                for n in range(2):
                    part[2 * p + t, pl.ds(m // 128 + n, width, stride=lines), :] = (
                        sums[t * width:(t + 1) * width, n * 128:(n + 1) * 128]
                    )
        for t in range(2):
            i = 2 * p + t

            @pl.when(jnp.logical_not(is_mine(i)))
            def _():
                core_copy(i).start()

    def add_core(i):
        @pl.when(is_mine(i))
        def _():
            core_copy(i).wait_recv()
            part[i] = part[i] + core_in[i]
            for copy in x1_copies(i):
                copy.start()

    def add_x1(i):
        @pl.when(is_mine(i))
        def _():
            copies, later = x1_copies(i), x2_copies(i)
            for n, to in enumerate((x_right, x_left)):
                copies[n].wait_recv()
                spot = lines_of(to, n * piece // 2, piece // 2)
                part[i, spot, :] = part[i, spot, :] + x1_in[i, n]
                later[n].start()

    def add_x2(i):
        @pl.when(is_mine(i))
        def _():
            for copy in x2_copies(i):
                copy.wait_recv()
            y_out[i] = part[i, lines_of(x, 0, piece), :] + (x2_in[i, 0] + x2_in[i, 1])
            for n in range(units):
                copy, owner, spot = y_copy(i, n)

                @pl.when(owner == l)
                def _():
                    y_in[spot, y] = y_out[i, pl.ds(n * unit, unit), :]

                @pl.when(owner != l)
                def _():
                    copy.start()

    def drain(i):
        @pl.when(pick(i, onward) > 0)
        def _():
            for h in range(2):
                onward_copy(i, h).wait_send()

        mine = is_mine(i)

        @pl.when(jnp.logical_not(mine))
        def _():
            core_copy(i).wait_send()

        @pl.when(mine)
        def _():
            for copy in x1_copies(i) + x2_copies(i):
                copy.wait_send()
            for n in range(units):
                copy, owner, _spot = y_copy(i, n)

                @pl.when(owner != l)
                def _():
                    copy.wait_send()

    def both(stage, p):
        for t in range(2):
            stage(2 * p + t)

    stages = ((1, add_core), (2, add_x1), (3, add_x2))

    def step(p, _):
        for t in range(2):
            i = 2 * p + t

            @pl.when(i > 0)
            def _():
                for h in range(2):
                    spot = buf.at[i, pl.ds(h * half, half)]
                    pltpu.make_async_copy(spot, spot, ring_rx.at[i, h]).wait()

                    @pl.when(pick(i, onward) > 0)
                    def _():
                        onward_copy(i, h).start()

        compute(p)
        for lag, stage in stages:
            @pl.when(p >= lag)
            def _():
                both(stage, p - lag)

        return 0

    lax.fori_loop(0, pairs - 2, step, 0)

    flag_core.wait()
    flag[1] = flag[0] + flag_c[...]
    for copy in flag_xs:
        copy.start()
    lax.fori_loop(pairs - 2, pairs - 1, step, 0)
    total_x = flag[1]
    for n, copy in enumerate(flag_xs):
        copy.wait()
        total_x = total_x + flag_x[n]
    flag[2] = total_x
    for copy in flag_ys:
        copy.start()
    lax.fori_loop(pairs - 1, pairs, step, 0)

    last = pairs - 1
    both(add_core, last)
    both(add_x1, last - 1)
    if last >= 2:
        both(add_x2, last - 2)
    both(add_x1, last)
    both(add_x2, last - 1)

    def drain_item(i, _):
        drain(i)
        return 0

    lax.fori_loop(0, nz - 4, drain_item, 0)
    both(add_x2, last)
    lax.fori_loop(nz - 4, nz, drain_item, 0)
    total_y = flag[2]
    for n, copy in enumerate(flag_ys):
        copy.wait()
        total_y = total_y + flag_y[n]
    flag_out[...] = total_y
    for copy in own_copies:
        copy.wait_send()

    for spot in range(per_owner):
        from_x = lax.rem(l * owned + spot * UNIT, width) // (width // NX)
        for i in range(NY):
            @pl.when(jnp.logical_not(jnp.logical_and(from_x == x, i == y)))
            def _():
                here = y_in.at[spot, i]
                pltpu.make_async_copy(here, here, y_rx.at[spot, i]).wait()
        total = y_in[spot, 0]
        for i in range(1, NY):
            total = total + y_in[spot, i]
        fin[pl.ds(spot * unit, unit), :] = total
    for n in range(lines):
        out[:, pl.ds(n * 128, 128)] = fin[pl.ds(n, owned, stride=lines), :]


def sparse_product(nz, a_panel, b_panel, a_occ, b_occ):
    rows, depth = a_panel.shape
    width = b_panel.shape[1]
    blocks = depth // BLOCK
    slots = blocks // 2
    lines = rows // 128
    owned = nz * width // (2 * NX * NY)
    piece = width // NX * lines
    unit = UNIT * lines
    columns = b_occ.shape[1]
    dma = pltpu.SemaphoreType.DMA
    f32, bf16 = jnp.float32, jnp.bfloat16
    scratch = [
        pltpu.VMEM((rows, depth), bf16),
        pltpu.VMEM((width, depth), bf16),
        pltpu.SMEM(a_occ.shape, jnp.int32),
        pltpu.SMEM((columns, blocks), jnp.int32),
        pltpu.VMEM((columns, blocks, 16, BLOCK), bf16),
        pltpu.VMEM((columns, blocks, 16, BLOCK), bf16),
        pltpu.VMEM((2 * width, depth), bf16),
        pltpu.VMEM((nz, width, slots * BLOCK), bf16),
        pltpu.VMEM((nz, width * lines, 128), f32),
        pltpu.VMEM((nz, width * lines, 128), f32),
        pltpu.VMEM((nz, 2, piece // 2, 128), f32),
        pltpu.VMEM((nz, 2, piece, 128), f32),
        pltpu.VMEM((nz, piece, 128), f32),
        pltpu.VMEM((owned // UNIT, NY, unit, 128), f32),
        pltpu.VMEM((owned * lines, 128), f32),
        pltpu.VMEM((3, 8, 128), f32),
        pltpu.VMEM((8, 128), f32),
        pltpu.VMEM((NX - 1, 8, 128), f32),
        pltpu.VMEM((NY - 1, 8, 128), f32),
        dma((4,)), dma((2, 2)), dma((nz, 2)), dma((nz, 2)),
        dma((nz,)), dma((nz,)), dma((nz, 2)), dma((nz, 2)), dma((nz, 2)), dma((nz, 2)),
        dma((nz, piece // unit)), dma((owned // UNIT, NY)),
        dma(()), dma(()), dma((NX - 1,)), dma((NX - 1,)), dma((NY - 1,)), dma((NY - 1,)),
    ]
    anywhere = pl.BlockSpec(memory_space=pl.ANY)
    inside = pl.BlockSpec(memory_space=pltpu.VMEM)
    return pl.pallas_call(
        functools.partial(kernel, nz, slots),
        out_shape=(jax.ShapeDtypeStruct((owned, rows), f32), jax.ShapeDtypeStruct((8, 128), f32)),
        in_specs=[anywhere] * 4,
        out_specs=(inside, inside),
        scratch_shapes=scratch,
        compiler_params=pltpu.CompilerParams(
            collective_id=0, has_side_effects=True, vmem_limit_bytes=60 * 1024 * 1024
        ),
        cost_estimate=pl.CostEstimate(
            flops=2 * rows * slots * BLOCK * nz * width, bytes_accessed=rows * depth * 2, transcendentals=0
        ),
    )(a_panel, b_panel.T, a_occ, b_occ.T)


def expand(occupancy, block):
    return jnp.repeat(jnp.repeat(occupancy, block, 0), block, 1).astype(jnp.bfloat16)


def dense_product(nz, a_panel, b_panel, a_occ, b_occ):
    z = lax.axis_index("row")
    width, depth = b_panel.shape[1], b_panel.shape[0]

    def step(s, carry):
        held, gathered = carry
        gathered = lax.dynamic_update_slice(gathered, held[None], (lax.rem(z - s + nz, nz), 0, 0))
        return lax.ppermute(held, "row", [(i, (i + 1) % nz) for i in range(nz)]), gathered

    occupied = lax.dynamic_slice_in_dim(b_occ.T, (z * width) // BLOCK, 1).astype(b_panel.dtype)
    start = (b_panel.T * jnp.repeat(occupied, BLOCK, 1), jnp.zeros((nz, width, depth), b_panel.dtype))
    _, gathered = lax.fori_loop(0, nz, step, start)
    terms = lax.dot_general(
        gathered.reshape(nz * width, depth),
        a_panel * expand(a_occ, BLOCK),
        (((1,), (1,)), ((), ())), preferred_element_type=jnp.float32,
    )
    shares = 2 * NX * NY
    terms = terms.reshape(shares, nz * width // shares, a_panel.shape[0])
    return lax.all_to_all(terms, ("col", "layer"), 0, 0).sum(0).T


def body(nz, a_panel, b_panel, a_occ, b_occ):
    result, over = sparse_product(nz, a_panel, b_panel, a_occ, b_occ)
    return lax.cond(
        over[0, 0] > 0,
        lambda: dense_product(nz, a_panel, b_panel, a_occ, b_occ),
        lambda: result.T,
    )


def solution(mesh):
    in_specs = (
        P("row", ("col", "layer")),
        P(("col", "layer"), "row"),
        P("row", ("col", "layer")),
        P(("col", "layer"), None),
    )
    out_specs = P("row", ("col", "layer"))
    return jax.shard_map(
        functools.partial(body, mesh.shape["row"]),
        mesh=mesh, in_specs=in_specs, out_specs=out_specs, check_vma=False,
    )
```

```python
import functools

import jax
import jax.numpy as jnp
from jax import lax
from jax.experimental import pallas as pl
from jax.experimental.pallas import tpu as pltpu
from jax.sharding import PartitionSpec as P

MESH = pl.DeviceIdType.MESH
BLOCK = 128
NX, NY = 4, 8


def ring_order(nz):
    if nz == 12:
        names = ["o0", "b1", "b2", "f1", "b3", "b4", "f2", "b5", "f3", "b6", "f4", "b7"]
    else:
        back = nz // 2
        names = ["o0"] + [n + str(s) for s in range(1, back + 1) for n in "bf" if s <= (nz - 1 - back if n == "f" else back)]
    items = [(n[0], int(n[1:])) for n in names]
    place = {item: i for i, item in enumerate(items)}
    offsets = [s if n != "f" else nz - s for n, s in items]
    onward = [place.get((n, s + 1), 0) for n, s in items]
    forward = [int(n == "f") for n, s in items]
    return offsets, onward, forward, place[("f", 1)], place[("b", 1)]


def pick(i, values):
    result = jnp.int32(values[0])
    for k, value in enumerate(values):
        if k > 0:
            result = jnp.where(i == k, jnp.int32(value), result)
    return result


def kernel(nz, slots, a_hbm, b_hbm, aocc_hbm, bocc_hbm, out, flag_out, a_v, b_v, aocc, bocc, stored, absent, wide, buf,
           part, core_in, x1_in, x2_in, y_out, y_in, f_out, fin, flag, flag_c, flag_x, flag_y,
           load_sem, own_tx, ring_tx, ring_rx, core_tx, core_rx, x1_tx, x1_rx, x2_tx, x2_rx,
           y_tx, y_rx, f_tx, f_rx, fc_tx, fc_rx, fx_tx, fx_rx, fy_tx, fy_rx):
    offsets, onward, forward, first_f, first_b = ring_order(nz)
    layers = NX * NY
    z, c, l = (lax.axis_index(name) for name in ("row", "col", "layer"))
    y, x = l // NX, lax.rem(l, NX)
    right, left = lax.rem(z + 1, nz), lax.rem(z + nz - 1, nz)
    rows, depth = a_v.shape
    width = b_v.shape[0]
    half = width // 2
    blocks = depth // BLOCK
    lines = rows // 128
    piece = width // NX * lines
    pair = piece // NY
    owned = out.shape[0]

    loads = [
        pltpu.make_async_copy(bocc_hbm, bocc, load_sem.at[0]),
        pltpu.make_async_copy(b_hbm, b_v, load_sem.at[1]),
        pltpu.make_async_copy(aocc_hbm, aocc, load_sem.at[2]),
        pltpu.make_async_copy(a_hbm, a_v, load_sem.at[3]),
    ]
    for copy in loads:
        copy.start()

    barrier = pltpu.get_barrier_semaphore()

    def greet(device):
        pl.semaphore_signal(barrier, inc=1, device_id=device, device_id_type=MESH)

    greet((right, c, l))
    greet((left, c, l))
    greet((z, 1 - c, l))

    def greet_layer(i, _):
        greet((z, c, lax.rem(l + i, layers)))
        return 0

    lax.fori_loop(1, layers, greet_layer, 0)

    def factor(value):
        return jnp.full((16, 128), value.astype(jnp.float32), jnp.float32).astype(jnp.bfloat16)

    own_column = (z * width) // BLOCK

    def note_blocks(n, over):
        count = jnp.int32(0)
        for k in range(blocks):
            stored[n, k] = factor(bocc[n, k])
            absent[n, k] = factor(1 - bocc[n, k])
            count = count + bocc[n, k]
        return over + jnp.maximum(count - slots, 0)

    loads[0].wait()
    note_blocks(own_column, jnp.int32(0))

    loads[1].wait()
    tiles = (width // 16, 16, BLOCK)
    held = [jnp.zeros(tiles, jnp.bfloat16)] * slots
    for k in reversed(range(blocks)):
        on, off = stored[own_column, k][None], absent[own_column, k][None]
        tile = b_v[:, k * BLOCK:(k + 1) * BLOCK].reshape(tiles)
        held = [(tile if s == 0 else held[s - 1]) * on + held[s] * off for s in range(slots)]
    for s in range(slots):
        buf[0, :, s * BLOCK:(s + 1) * BLOCK] = held[s].reshape(width, BLOCK)

    def mask_a(k, _):
        cols = pl.ds(pl.multiple_of(k * BLOCK, BLOCK), BLOCK)
        for i in range(rows // BLOCK):
            mask = factor(aocc[i, k])
            tile = a_v[pl.ds(i * BLOCK, BLOCK), cols].reshape(BLOCK // 16, 16, BLOCK)
            a_v[pl.ds(i * BLOCK, BLOCK), cols] = (tile * mask[None]).reshape(BLOCK, BLOCK)
        return 0

    def prepare():
        loads[2].wait()
        loads[3].wait()
        lax.fori_loop(0, blocks, mask_a, 0)
        over = lax.fori_loop(0, bocc.shape[0], note_blocks, jnp.int32(0))
        flag[0] = jnp.full(flag.shape[1:], over.astype(jnp.float32), jnp.float32)

    early = z < nz // 2
    pl.when(early)(prepare)
    pl.semaphore_wait(barrier, layers + 2)

    def ring_copy(i, h, to, device, tx):
        return pltpu.make_async_remote_copy(
            src_ref=buf.at[i, pl.ds(h * half, half)], dst_ref=buf.at[to, pl.ds(h * half, half)],
            send_sem=tx, recv_sem=ring_rx.at[to, h],
            device_id=(device, c, l), device_id_type=MESH,
        )

    def onward_copy(i, h):
        device = jnp.where(pick(i, forward) > 0, right, left)
        return ring_copy(i, h, pick(i, onward), device, ring_tx.at[i, h])

    own_copies = [ring_copy(0, h, first_b, left, own_tx.at[0, h]) for h in range(2)]
    own_copies += [ring_copy(0, h, first_f, right, own_tx.at[1, h]) for h in range(2)]
    for copy in own_copies:
        copy.start()

    flag_core = pltpu.make_async_remote_copy(
        src_ref=flag.at[0], dst_ref=flag_c, send_sem=fc_tx, recv_sem=fc_rx,
        device_id=(z, 1 - c, l), device_id_type=MESH,
    )

    def flag_copies(i, inbox, count, tx, rx, device):
        return [
            pltpu.make_async_remote_copy(
                src_ref=flag.at[i], dst_ref=inbox.at[n - 1], send_sem=tx.at[n - 1], recv_sem=rx.at[n - 1],
                device_id=(z, c, device(n)), device_id_type=MESH,
            )
            for n in range(1, count)
        ]

    flag_xs = flag_copies(1, flag_x, NX, fx_tx, fx_rx, lambda n: y * NX + lax.rem(x + n, NX))
    flag_ys = flag_copies(2, flag_y, NY, fy_tx, fy_rx, lambda n: lax.rem(y + n, NY) * NX + x)

    pl.when(jnp.logical_not(early))(prepare)
    flag_core.start()

    def shard(i):
        return lax.rem(z + pick(i, offsets), nz)

    def is_mine(i):
        return shard(i) // (nz // 2) == c

    def lines_of(p, start, size):
        return pl.ds(pl.multiple_of(p * piece + start, 8), size)

    x_right, x_left, x_far = (lax.rem(x + n, NX) for n in (1, NX - 1, 2))

    def core_copy(i):
        return pltpu.make_async_remote_copy(
            src_ref=part.at[i], dst_ref=core_in.at[i], send_sem=core_tx.at[i], recv_sem=core_rx.at[i],
            device_id=(z, 1 - c, l), device_id_type=MESH,
        )

    def x1_copies(i):
        return [
            pltpu.make_async_remote_copy(
                src_ref=part.at[i, lines_of(x_far, n * piece // 2, piece // 2)], dst_ref=x1_in.at[i, n],
                send_sem=x1_tx.at[i, n], recv_sem=x1_rx.at[i, n],
                device_id=(z, c, y * NX + to), device_id_type=MESH,
            )
            for n, to in enumerate((x_right, x_left))
        ]

    def x2_copies(i):
        return [
            pltpu.make_async_remote_copy(
                src_ref=part.at[i, lines_of(to, 0, piece)], dst_ref=x2_in.at[i, n],
                send_sem=x2_tx.at[i, n], recv_sem=x2_rx.at[i, n],
                device_id=(z, c, y * NX + to), device_id_type=MESH,
            )
            for n, to in enumerate((x_right, x_left))
        ]

    def y_copies(i):
        copies = []
        for n in range(1, NY):
            to = lax.rem(y + n, NY)
            copies.append(pltpu.make_async_remote_copy(
                src_ref=y_out.at[i, pl.ds(pl.multiple_of(to * pair, 8), pair)], dst_ref=y_in.at[i, n - 1],
                send_sem=y_tx.at[i, n - 1], recv_sem=y_rx.at[i, n - 1],
                device_id=(z, c, to * NX + x), device_id_type=MESH,
            ))
        return copies

    def f_copy(i):
        column = width * lax.rem(shard(i), nz // 2) + (width // NX) * x + (pair // lines) * y
        owner, spot = column // owned, lax.rem(column, owned) // (pair // lines)
        copy = pltpu.make_async_remote_copy(
            src_ref=f_out.at[i], dst_ref=fin.at[pl.ds(pl.multiple_of(spot * pair, 8), pair)],
            send_sem=f_tx.at[i], recv_sem=f_rx.at[spot],
            device_id=(z, c, owner), device_id_type=MESH,
        )
        return copy, owner, spot

    def compute(i):
        column = (shard(i) * width) // BLOCK
        held = [buf[i, :, s * BLOCK:(s + 1) * BLOCK].reshape(tiles) for s in range(slots)]
        for k in range(blocks):
            on, off = stored[column, k][None], absent[column, k][None]
            wide[:, k * BLOCK:(k + 1) * BLOCK] = (held[0] * on).reshape(width, BLOCK)
            held = [
                held[s] * off + held[s + 1] * on if s < slots - 1 else held[s] * off
                for s in range(min(slots, blocks - 1 - k))
            ]
        lhs = wide[...]
        for m in range(0, rows, 256):
            sums = lax.dot_general(
                lhs, a_v[pl.ds(m, 256), :], (((1,), (1,)), ((), ())), preferred_element_type=jnp.float32,
            )
            for n in range(2):
                part[i, pl.ds(m // 128 + n, width, stride=lines), :] = sums[:, n * 128:(n + 1) * 128]

        @pl.when(jnp.logical_not(is_mine(i)))
        def _():
            core_copy(i).start()

    def add_core(i):
        @pl.when(is_mine(i))
        def _():
            core_copy(i).wait_recv()
            part[i] = part[i] + core_in[i]
            for copy in x1_copies(i):
                copy.start()

    def add_x1(i):
        @pl.when(is_mine(i))
        def _():
            copies, later = x1_copies(i), x2_copies(i)
            for n, to in enumerate((x_right, x_left)):
                copies[n].wait_recv()
                spot = lines_of(to, n * piece // 2, piece // 2)
                part[i, spot, :] = part[i, spot, :] + x1_in[i, n]
                later[n].start()

    def add_x2(i):
        @pl.when(is_mine(i))
        def _():
            for copy in x2_copies(i):
                copy.wait_recv()
            y_out[i] = part[i, lines_of(x, 0, piece), :] + (x2_in[i, 0] + x2_in[i, 1])
            for copy in y_copies(i):
                copy.start()

    def add_y(i):
        @pl.when(is_mine(i))
        def _():
            total = y_out[i, pl.ds(pl.multiple_of(y * pair, 8), pair), :]
            for n, copy in enumerate(y_copies(i)):
                copy.wait_recv()
                total = total + y_in[i, n]
            copy, owner, spot = f_copy(i)
            f_out[i] = total

            @pl.when(owner == l)
            def _():
                fin[pl.ds(pl.multiple_of(spot * pair, 8), pair), :] = total

            @pl.when(owner != l)
            def _():
                copy.start()

    def drain(i):
        @pl.when(pick(i, onward) > 0)
        def _():
            for h in range(2):
                onward_copy(i, h).wait_send()

        mine = is_mine(i)

        @pl.when(jnp.logical_not(mine))
        def _():
            core_copy(i).wait_send()

        @pl.when(mine)
        def _():
            for copy in x1_copies(i) + x2_copies(i) + y_copies(i):
                copy.wait_send()
            copy, owner, _spot = f_copy(i)

            @pl.when(owner != l)
            def _():
                copy.wait_send()

    stages = ((1, add_core), (3, add_x1), (5, add_x2), (8, add_y))

    def step(i, _):
        @pl.when(i > 0)
        def _():
            for h in range(2):
                spot = buf.at[i, pl.ds(h * half, half)]
                pltpu.make_async_copy(spot, spot, ring_rx.at[i, h]).wait()

                @pl.when(pick(i, onward) > 0)
                def _():
                    onward_copy(i, h).start()

        compute(i)
        for lag, stage in stages:
            @pl.when(i >= lag)
            def _():
                stage(i - lag)

        return 0

    lax.fori_loop(0, nz - 2, step, 0)

    flag_core.wait()
    flag[1] = flag[0] + flag_c[...]
    for copy in flag_xs:
        copy.start()
    lax.fori_loop(nz - 2, nz - 1, step, 0)
    total_x = flag[1]
    for n, copy in enumerate(flag_xs):
        copy.wait()
        total_x = total_x + flag_x[n]
    flag[2] = total_x
    for copy in flag_ys:
        copy.start()
    lax.fori_loop(nz - 1, nz, step, 0)

    def catch_up(k, low, high):
        for i in range(max(low, 0), high):
            stages[k][1](i)

    left_over = [nz - lag for lag, _stage in stages]
    add_core(nz - 1)
    catch_up(1, left_over[1], nz - 1)
    catch_up(2, left_over[2], nz - 3)
    catch_up(3, left_over[3], nz - 6)
    add_x1(nz - 1)
    catch_up(2, max(left_over[2], nz - 3), nz - 1)
    catch_up(3, max(left_over[3], nz - 6), nz - 4)
    add_x2(nz - 1)
    catch_up(3, max(left_over[3], nz - 4), nz - 1)
    for i in range(nz - 1):
        drain(i)
    add_y(nz - 1)
    drain(nz - 1)
    total_y = flag[2]
    for n, copy in enumerate(flag_ys):
        copy.wait()
        total_y = total_y + flag_y[n]
    flag_out[0, 0] = jnp.where(jnp.max(total_y) > 0, jnp.int32(1), jnp.int32(0))
    for copy in own_copies:
        copy.wait_send()

    for spot in range(owned * lines // pair):
        column = lax.rem(l * owned + spot * (pair // lines), width)
        from_x, from_y = column // (width // NX), lax.rem(column, width // NX) // (pair // lines)

        @pl.when(jnp.logical_not(jnp.logical_and(from_x == x, from_y == y)))
        def _():
            here = fin.at[pl.ds(spot * pair, pair)]
            pltpu.make_async_copy(here, here, f_rx.at[spot]).wait()
    for n in range(lines):
        out[:, pl.ds(n * 128, 128)] = fin[pl.ds(n, owned, stride=lines), :]


def sparse_product(nz, a_panel, b_panel, a_occ, b_occ):
    rows, depth = a_panel.shape
    width = b_panel.shape[1]
    blocks = depth // BLOCK
    slots = blocks // 2
    lines = rows // 128
    owned = nz * width // (2 * NX * NY)
    piece = width // NX * lines
    pair = piece // NY
    columns = b_occ.shape[1]
    dma = pltpu.SemaphoreType.DMA
    f32, bf16 = jnp.float32, jnp.bfloat16
    scratch = [
        pltpu.VMEM((rows, depth), bf16),
        pltpu.VMEM((width, depth), bf16),
        pltpu.SMEM(a_occ.shape, jnp.int32),
        pltpu.SMEM((columns, blocks), jnp.int32),
        pltpu.VMEM((columns, blocks, 16, BLOCK), bf16),
        pltpu.VMEM((columns, blocks, 16, BLOCK), bf16),
        pltpu.VMEM((width, depth), bf16),
        pltpu.VMEM((nz, width, slots * BLOCK), bf16),
        pltpu.VMEM((nz, width * lines, 128), f32),
        pltpu.VMEM((nz, width * lines, 128), f32),
        pltpu.VMEM((nz, 2, piece // 2, 128), f32),
        pltpu.VMEM((nz, 2, piece, 128), f32),
        pltpu.VMEM((nz, piece, 128), f32),
        pltpu.VMEM((nz, NY - 1, pair, 128), f32),
        pltpu.VMEM((nz, pair, 128), f32),
        pltpu.VMEM((owned * lines, 128), f32),
        pltpu.VMEM((3, 8, 128), f32),
        pltpu.VMEM((8, 128), f32),
        pltpu.VMEM((NX - 1, 8, 128), f32),
        pltpu.VMEM((NY - 1, 8, 128), f32),
        dma((4,)), dma((2, 2)), dma((nz, 2)), dma((nz, 2)),
        dma((nz,)), dma((nz,)), dma((nz, 2)), dma((nz, 2)), dma((nz, 2)), dma((nz, 2)),
        dma((nz, NY - 1)), dma((nz, NY - 1)), dma((nz,)), dma((owned * lines // pair,)),
        dma(()), dma(()), dma((NX - 1,)), dma((NX - 1,)), dma((NY - 1,)), dma((NY - 1,)),
    ]
    anywhere = pl.BlockSpec(memory_space=pl.ANY)
    inside = pl.BlockSpec(memory_space=pltpu.VMEM)
    return pl.pallas_call(
        functools.partial(kernel, nz, slots),
        out_shape=(jax.ShapeDtypeStruct((owned, rows), f32), jax.ShapeDtypeStruct((1, 1), jnp.int32)),
        in_specs=[anywhere] * 4,
        out_specs=(inside, pl.BlockSpec(memory_space=pltpu.SMEM)),
        scratch_shapes=scratch,
        compiler_params=pltpu.CompilerParams(
            collective_id=0, has_side_effects=True, vmem_limit_bytes=60 * 1024 * 1024
        ),
        cost_estimate=pl.CostEstimate(
            flops=2 * rows * slots * BLOCK * nz * width, bytes_accessed=rows * depth * 2, transcendentals=0
        ),
    )(a_panel, b_panel.T, a_occ, b_occ.T)


def expand(occupancy, block):
    return jnp.repeat(jnp.repeat(occupancy, block, 0), block, 1).astype(jnp.bfloat16)


def dense_product(nz, a_panel, b_panel, a_occ, b_occ):
    z = lax.axis_index("row")
    width, depth = b_panel.shape[1], b_panel.shape[0]

    def step(s, carry):
        held, gathered = carry
        gathered = lax.dynamic_update_slice(gathered, held[None], (lax.rem(z - s + nz, nz), 0, 0))
        return lax.ppermute(held, "row", [(i, (i + 1) % nz) for i in range(nz)]), gathered

    occupied = lax.dynamic_slice_in_dim(b_occ.T, (z * width) // BLOCK, 1).astype(b_panel.dtype)
    start = (b_panel.T * jnp.repeat(occupied, BLOCK, 1), jnp.zeros((nz, width, depth), b_panel.dtype))
    _, gathered = lax.fori_loop(0, nz, step, start)
    terms = lax.dot_general(
        gathered.reshape(nz * width, depth),
        a_panel * expand(a_occ, BLOCK),
        (((1,), (1,)), ((), ())), preferred_element_type=jnp.float32,
    )
    shares = 2 * NX * NY
    terms = terms.reshape(shares, nz * width // shares, a_panel.shape[0])
    return lax.all_to_all(terms, ("col", "layer"), 0, 0).sum(0).T


def body(nz, a_panel, b_panel, a_occ, b_occ):
    result, over = sparse_product(nz, a_panel, b_panel, a_occ, b_occ)
    return lax.cond(
        over[0, 0] > 0,
        lambda: dense_product(nz, a_panel, b_panel, a_occ, b_occ),
        lambda: result.T,
    )


def solution(mesh):
    in_specs = (
        P("row", ("col", "layer")),
        P(("col", "layer"), "row"),
        P("row", ("col", "layer")),
        P(("col", "layer"), None),
    )
    out_specs = P("row", ("col", "layer"))
    return jax.shard_map(
        functools.partial(body, mesh.shape["row"]),
        mesh=mesh, in_specs=in_specs, out_specs=out_specs, check_vma=False,
    )
```
